32 devices in a mesh: depth: 4 (over y, x), lat: 8 (over z, core).
Axes of the slice: x: 2, y: 2, z: 4, core: 2. Of those that a mesh axis runs over, the one named last changes fastest.
Arguments:
- probe: bfloat16 [2, 256, 256], replicated, may hold values from -6 to 6
- positions: int32 [2, 32, 2], P(None, 'lat'), may hold values from 0 to 255
- object_phase: bfloat16 [4, 2048, 512], P('depth', 'lat'), may hold values from -3.140625 to 3.140625
- propagator: float32 [256, 256], replicated, may hold values from -3.140625 to 3.140625
- stored: bfloat16 [4, 32, 2, 256, 256], P('depth', 'lat'), may hold values from -6 to 6
- measured: float32 [32, 256, 256], P('lat'), may hold values from 0 to 2
Outputs:
- leaving: bfloat16 [4, 32, 2, 256, 256], P('depth', 'lat')
- gradient: float32 [4, 2, 2048, 512], P('depth', None, 'lat')
The draws below stay inside these ranges and needn't reach their ends.
Inputs may be any that keep to these rules, and one draw needn't show every extreme that they name: positions[d, q, 0] and positions[d, q, 1] are the row and column of the corner of probe q's window inside the tile of probe q; windows reach into the next tile's first rows.
All inputs are finite; a program needn't handle non-finite values.
Results may differ from the reference program's by a relative error of at most 0.04.
Values may be sent and summed in bfloat16 or wider, within the bound.
A program may use at most 64 MiB of HBM per device.

```python
import math
import jax
import jax.numpy as jnp
from jax import lax

NPIX = 256
SLICES = 1
TX = 256
PROBES = 4
COLS = 512
ROWS = 2048
LAYERS = 4
PROBES_ALL = 32
N_DEPTH = 4


def place_ends(array, own_key, smallest, largest):
    shape = array.shape
    spot = [jax.random.randint(jax.random.fold_in(own_key, axis), (), 0, shape[axis]) for axis in range(len(shape))]
    array = array.at[tuple(spot)].set(smallest)
    longest = shape.index(max(shape))
    spot[longest] = (spot[longest] + 1) % shape[longest]
    return array.at[tuple(spot)].set(largest)


def level_of(own_key, dims, split, least, largest):
    loudness = 1.0
    for axis_at, shards_of in split:
        heights = jax.random.uniform(jax.random.fold_in(jax.random.fold_in(own_key, 6), axis_at), (shards_of,), jnp.float32, least / len(split), largest / len(split))
        loudness = loudness * jnp.repeat(jnp.exp(heights), dims[axis_at] // shards_of).reshape((-1,) + (1,) * (len(dims) - 1 - axis_at))
    return loudness


def scatter_about(stream_key, extent, scale, limit, shards=(), kind=jnp.bfloat16):
    values = jax.random.normal(stream_key, extent, jnp.float32) * scale
    if len(shards) > 0:
        values = level_of(stream_key, extent, shards, -0.22, 0.18) * values
    return jnp.clip(values, min=-limit, max=limit).astype(kind)


def setup_inputs(seed: int = 0) -> dict:
    keys = jax.random.split(jax.random.key(seed), 7)
    probe = scatter_about(keys[0], (2, NPIX, NPIX), 1.0, 6.0)
    positions = place_ends(jax.random.randint(keys[1], (2, PROBES_ALL, 2), 0, TX), jax.random.fold_in(keys[1], 1), 0, TX - 1).astype(jnp.int32)
    object_phase = jnp.clip(jax.random.uniform(keys[2], (LAYERS, ROWS, COLS), jnp.float32, -3.140625, 3.140625), -3.140625, 3.140625).astype(jnp.bfloat16)
    propagator = jnp.clip(jax.random.uniform(keys[3], (NPIX, NPIX), jnp.float32, -3.140625, 3.140625), -3.140625, 3.140625)
    stored = scatter_about(keys[4], (N_DEPTH, PROBES_ALL, 2, NPIX, NPIX), 1.0, 6.0, ((0, 4), (1, 8)))
    measured = jnp.clip(2.0 * jax.random.uniform(keys[5], (PROBES_ALL, NPIX, NPIX), jnp.float32) ** level_of(keys[5], (PROBES_ALL, NPIX, NPIX), ((0, 8),), -0.2, 0.2), 0.0, 2.0)
    return dict(probe=probe, positions=positions, object_phase=object_phase, propagator=propagator, stored=stored, measured=measured)


def tables():
    counter = jnp.arange(NPIX, dtype=jnp.int32)
    product = counter[:, None] * counter[None, :] % NPIX
    angles = 2.0 * math.pi / NPIX * product.astype(jnp.float32)
    factor = 1.0 / math.sqrt(NPIX)
    real_part = jnp.cos(angles) * factor
    imag_part = -jnp.sin(angles) * factor
    forward = jnp.stack([jnp.stack([real_part, -imag_part]), jnp.stack([imag_part, real_part])]).astype(jnp.bfloat16)
    inverse = jnp.stack([jnp.stack([real_part, imag_part]), jnp.stack([-imag_part, real_part])]).astype(jnp.bfloat16)
    return (forward, inverse)

def transform(table, waves):
    left = jnp.einsum('abjk,pbkl->pajl', table.astype(jnp.float32), waves.astype(jnp.float32)).astype(jnp.bfloat16)
    return jnp.einsum('pbjk,abkl->pajl', left.astype(jnp.float32), table.astype(jnp.float32))

def times(first, second):
    first = first.astype(jnp.float32)
    second = second.astype(jnp.float32)
    real_part = first[..., 0, :, :] * second[..., 0, :, :] - first[..., 1, :, :] * second[..., 1, :, :]
    imag_part = first[..., 0, :, :] * second[..., 1, :, :] + first[..., 1, :, :] * second[..., 0, :, :]
    return jnp.stack([real_part, imag_part], axis=-3)

def conj_times(first, second):
    first = first.astype(jnp.float32)
    second = second.astype(jnp.float32)
    real_part = first[..., 0, :, :] * second[..., 0, :, :] + first[..., 1, :, :] * second[..., 1, :, :]
    imag_part = first[..., 0, :, :] * second[..., 1, :, :] - first[..., 1, :, :] * second[..., 0, :, :]
    return jnp.stack([real_part, imag_part], axis=-3)

def slice_forward(wave, transmit, kernel, forward, inverse):
    exited = times(wave, transmit).astype(jnp.bfloat16)
    spectrum = transform(forward, exited)
    shifted = times(kernel, spectrum).astype(jnp.bfloat16)
    return transform(inverse, shifted).astype(jnp.bfloat16)

def slice_adjoint(adjoint, wave, transmit, kernel, forward, inverse):
    spectrum = transform(forward, adjoint)
    shifted = conj_times(kernel, spectrum).astype(jnp.bfloat16)
    exited = transform(inverse, shifted)
    term = conj_times(wave, exited)
    return (conj_times(transmit, exited).astype(jnp.bfloat16), term)

def far_adjoint(exit_wave, intensity, forward, inverse):
    field = transform(forward, exit_wave)
    power = field[..., 0, :, :] * field[..., 0, :, :] + field[..., 1, :, :] * field[..., 1, :, :]
    weight = (power - intensity)[..., None, :, :] * field
    return transform(inverse, weight.astype(jnp.bfloat16)).astype(jnp.bfloat16)

def windows(layer_phase, rows, cols):

    def single(row, col):
        return lax.dynamic_slice(layer_phase, (row, col), (NPIX, NPIX))
    cut = jax.vmap(single)(rows, cols).astype(jnp.float32)
    return jnp.stack([jnp.cos(cut), jnp.sin(cut)], axis=1)

def reference(probe, positions, object_phase, propagator, stored, measured):
    forward, inverse = tables()
    kernel = jnp.stack([jnp.cos(propagator), jnp.sin(propagator)])
    owner = jnp.arange(PROBES_ALL, dtype=jnp.int32) // PROBES
    ahead_rows = (owner * TX + positions[0, :, 0]).astype(jnp.int32)
    ahead_cols = positions[0, :, 1].astype(jnp.int32)
    behind_rows = (owner * TX + positions[1, :, 0]).astype(jnp.int32)
    behind_cols = positions[1, :, 1].astype(jnp.int32)
    extended = jnp.concatenate([object_phase, object_phase[:, :NPIX]], axis=1)
    sections = extended.reshape(N_DEPTH, SLICES, ROWS + NPIX, COLS)

    def ahead(wave, layers):
        for index in range(SLICES):
            wave = slice_forward(wave, windows(layers[index], ahead_rows, ahead_cols), kernel, forward, inverse)
        return (wave, wave)
    start = jnp.broadcast_to(probe, (PROBES_ALL, 2, NPIX, NPIX))
    _, leaving = lax.scan(ahead, start, sections)

    def replay(wave, layers):
        inputs = []
        transmits = []
        for index in range(SLICES):
            transmit = windows(layers[index], behind_rows, behind_cols)
            inputs.append(wave)
            transmits.append(transmit)
            wave = slice_forward(wave, transmit, kernel, forward, inverse)
        return (wave, inputs, transmits)
    last_exit, _, _ = replay(stored[N_DEPTH - 1], sections[N_DEPTH - 1])
    adjoint = far_adjoint(last_exit, measured, forward, inverse)

    def behind(adjoint, pair):
        layers, start_wave = pair
        _, inputs, transmits = replay(start_wave, layers)
        terms = [None] * SLICES
        for index in reversed(range(SLICES)):
            adjoint, terms[index] = slice_adjoint(adjoint, inputs[index], transmits[index], kernel, forward, inverse)
        return (adjoint, jnp.stack(terms))
    _, terms = lax.scan(behind, adjoint, (sections, stored), reverse=True)
    terms = terms.reshape(LAYERS, PROBES_ALL, 2, NPIX, NPIX)
    gradient = jnp.zeros((LAYERS, 2, ROWS + NPIX, COLS), jnp.float32)
    anchor = jnp.zeros((), jnp.int32)

    def place(probe_index, gradient):
        corner = (anchor, anchor, behind_rows[probe_index], behind_cols[probe_index])
        piece = lax.dynamic_slice(gradient, corner, (LAYERS, 2, NPIX, NPIX))
        piece = piece + lax.dynamic_index_in_dim(terms, probe_index, 1, False)
        return lax.dynamic_update_slice(gradient, piece, corner)
    gradient = lax.fori_loop(0, PROBES_ALL, place, gradient)
    folded = gradient[:, :, :ROWS].at[:, :, :NPIX].add(gradient[:, :, ROWS:])
    return (leaving, folded)
```

```python
import functools
import math

import jax
import jax.numpy as jnp
import numpy as np
from jax import lax
from jax.experimental import pallas as pl
from jax.experimental.pallas import tpu as pltpu
from jax.sharding import PartitionSpec as P

MESH = pl.DeviceIdType.MESH
F32 = jnp.float32
BF16 = jnp.bfloat16


def tables(n):
    counter = np.arange(n)
    angles = 2.0 * math.pi / n * (counter[:, None] * counter[None, :] % n)
    re = np.cos(angles) / math.sqrt(n)
    im = -np.sin(angles) / math.sqrt(n)
    ahead = np.block([[re, -im], [im, re]])
    back = np.block([[re, im], [-im, re]])
    return ahead.astype(BF16), back.astype(BF16)


def fit(function, terms):
    top = (math.pi + 1e-3) ** 2
    u = (np.cos(np.pi * (np.arange(400) + 0.5) / 400) + 1) * top / 2
    poly = np.polynomial.Chebyshev.fit(u, function(np.sqrt(u)), terms - 1, domain=[0, top])
    return [float(v) for v in poly.convert(kind=np.polynomial.Polynomial).coef]


SIN = fit(lambda x: np.sin(x) / x, 7)
COS = fit(np.cos, 8)


def horner(coefs, u):
    value = jnp.full_like(u, coefs[-1])
    for coef in coefs[-2::-1]:
        value = value * u + coef
    return value


def cos_sin(x):
    u = x * x
    return horner(COS, u), x * horner(SIN, u)


def rows_to_lanes(x):
    half = x.shape[0] // 2
    return jnp.concatenate([x[:half], x[half:]], axis=1)


def pair(re, im):
    return jnp.concatenate([re.astype(BF16), im.astype(BF16)], axis=0)


def kernel(D, N, Pn, pos, a_ref, b_ref, probe, tile, prop, stored, measured,
           leaving, grad,
           tiles, nexts, h_ref, waves, rolled, st3, ge_out, ge_in, own, nxt, rim_out, rim_in,
           t_send, t_recv, n_send, n_recv, s_send, s_recv, g_send, g_recv, r_send, r_recv):
    n = prop.shape[0]
    slots = st3.shape[0]
    d = lax.axis_index("depth")
    l = lax.axis_index("lat")
    before = lax.rem(l + N - 1, N)
    after = lax.rem(l + 1, N)

    def remote(src, dst, send, recv, depth, lat):
        return pltpu.make_async_remote_copy(
            src_ref=src, dst_ref=dst, send_sem=send, recv_sem=recv,
            device_id=(depth, lat), device_id_type=MESH)

    barrier = pltpu.get_barrier_semaphore()
    for off in range(1, D):
        pl.semaphore_signal(barrier, inc=1, device_id=(lax.rem(d + off, D), l), device_id_type=MESH)
    for other in (before, after):
        pl.semaphore_signal(barrier, inc=1, device_id=(d, other), device_id_type=MESH)
    pl.semaphore_wait(barrier, D + 1)

    def send_tile(j):
        return remote(tile, tiles.at[d], t_send.at[j], t_recv.at[d], j, l)

    def recv_tile(k):
        return remote(tile, tiles.at[k], t_send.at[k], t_recv.at[k], d, l)

    def pass_on(k, source):
        return remote(source, nexts.at[k], n_send.at[k], n_recv.at[k], d, before)

    def send_stored(q):
        return remote(stored.at[q], st3.at[q // D], s_send.at[q], s_recv.at[q // D], q % D, l)

    pass_on(d, tile).start()
    for off in range(1, D):
        send_tile(lax.rem(d + off, D)).start()

    @pl.when(d == D - 1)
    def _():
        for q in range(Pn):
            if q % D != D - 1:
                send_stored(q).start()
            else:
                st3[q // D] = stored[q]

    tiles[d] = tile[...]
    c, s = cos_sin(prop[...])
    h_ref[0] = c
    h_ref[1] = s

    row = lax.broadcasted_iota(jnp.int32, (n, n), 0)
    col = lax.broadcasted_iota(jnp.int32, (n, n), 1)

    def shift(lead, by):
        at = lead + by
        at = jnp.where(at < 0, at + n, at)
        return jnp.where(at >= n, at - n, at)

    def one_hot(where):
        return jnp.where(where, 1.0, 0.0).astype(BF16)

    def move(wave, left, right):
        turned = jnp.dot(wave, right, preferred_element_type=F32).astype(BF16)
        return (jnp.dot(left, turned[:n], preferred_element_type=F32).astype(BF16),
                jnp.dot(left, turned[n:], preferred_element_type=F32).astype(BF16))

    def roll_in(wave, r, c):
        left = one_hot(col == shift(row, -r))
        right = one_hot(row == shift(col, -c))
        return move(wave, left, right)

    def roll_out(wave, r, c):
        left = one_hot(col == shift(row, r))
        right = one_hot(row == shift(col, c))
        return move(wave, left, right)

    @pl.loop(0, Pn)
    def _(q):
        re, im = roll_in(probe[...].reshape(2 * n, n), pos[0, q, 0], pos[0, q, 1])
        waves[q, :n] = re
        waves[q, n:] = im
        re, im = roll_in(stored[q].reshape(2 * n, n), pos[1, q, 0], pos[1, q, 1])
        rolled[q, :n] = re
        rolled[q, n:] = im

    for off in range(1, D):
        k = lax.rem(d + off, D)
        recv_tile(k).wait_recv()
        pass_on(k, tiles.at[k]).start()
    for off in range(D):
        k = lax.rem(d + off, D)
        pass_on(k, tiles.at[k]).wait_recv()

    def dft(wave):
        left = jnp.dot(a_ref[...], wave, preferred_element_type=F32).astype(BF16)
        out = jnp.dot(rows_to_lanes(left), b_ref[...], preferred_element_type=F32)
        return out[:, :n], out[:, n:]

    def idft(wave):
        left = jnp.dot(b_ref[...], wave, preferred_element_type=F32).astype(BF16)
        out = jnp.dot(rows_to_lanes(left), a_ref[...], preferred_element_type=F32)
        return out[:, :n], out[:, n:]

    def transmission(k, r, c):
        right = col < c
        here = jnp.where(right, tiles[k, :, n:].astype(F32), tiles[k, :, :n].astype(F32))
        there = jnp.where(right, nexts[k, :, n:].astype(F32), nexts[k, :, :n].astype(F32))
        return cos_sin(jnp.where(row < r, there, here))

    def through(re, im, t):
        tr, ti = t
        fr, fi = dft(pair(re * tr - im * ti, re * ti + im * tr))
        hr, hi = h_ref[0], h_ref[1]
        return idft(pair(hr * fr - hi * fi, hr * fi + hi * fr))

    def send_ge(slot, k, q):
        return remote(ge_out.at[slot, k], ge_in.at[q], g_send.at[slot, k], g_recv.at[q], k, l)

    def backward(slot):
        q = slot * D + d
        r = pos[1, q, 0]
        c = pos[1, q, 1]

        @pl.when(d != D - 1)
        def _():
            remote(stored.at[q], st3.at[slot], s_send.at[q], s_recv.at[slot], d, l).wait_recv()

        re, im = roll_in(st3[slot].reshape(2 * n, n), r, c)
        xr, xi = through(re.astype(F32), im.astype(F32), transmission(D - 1, r, c))
        fr, fi = dft(pair(xr, xi))
        weight = fr * fr + fi * fi - measured[q]
        gr, gi = idft(pair(weight * fr, weight * fi))

        def step(i, g):
            k = D - 1 - i
            fr, fi = dft(g)
            hr, hi = h_ref[0], h_ref[1]
            er, ei = idft(pair(hr * fr + hi * fi, hr * fi - hi * fr))
            ge_out[slot, k] = pair(er, ei)

            @pl.when(k == d)
            def _():
                ge_in[q] = pair(er, ei)

            @pl.when(k != d)
            def _():
                send_ge(slot, k, q).start()

            tr, ti = transmission(k, r, c)
            return pair(tr * er + ti * ei, tr * ei - ti * er)

        lax.fori_loop(0, D, step, pair(gr, gi))

    for slot in range(slots):
        if (slot + 1) * D <= Pn:
            backward(slot)
        else:
            pl.when(slot * D + d < Pn)(functools.partial(backward, slot))

    def forward(k, _):
        def one(p, _):
            wave = waves[p].astype(F32)
            re, im = through(wave[:n], wave[n:], transmission(k, pos[0, p, 0], pos[0, p, 1]))
            waves[p] = pair(re, im)
            return 0

        return lax.fori_loop(0, Pn, one, 0)

    lax.fori_loop(0, d + 1, forward, 0)

    @pl.loop(0, Pn)
    def _(p):
        re, im = roll_out(waves[p], pos[0, p, 0], pos[0, p, 1])
        leaving[p, 0] = re
        leaving[p, 1] = im

    for q in range(Pn):
        @pl.when(d != q % D)
        def _():
            remote(ge_out.at[0, 0], ge_in.at[q], g_send.at[0, 0], g_recv.at[q], d, l).wait_recv()

        u = rolled[q].astype(F32)
        g = ge_in[q].astype(F32)
        ur, ui, gr, gi = u[:n], u[n:], g[:n], g[n:]
        lower = row < pos[1, q, 0]
        right = col < pos[1, q, 1]
        for part, term in enumerate((ur * gr + ui * gi, ur * gi - ui * gr)):
            here = jnp.where(lower, 0.0, term)
            there = jnp.where(lower, term, 0.0)
            for target, value in ((own, here), (nxt, there)):
                west = jnp.where(right, 0.0, value)
                east = jnp.where(right, value, 0.0)
                if q > 0:
                    west = west + target[part, :, :n]
                    east = east + target[part, :, n:]
                target[part, :, :n] = west
                target[part, :, n:] = east

    rim_out[...] = nxt[...].astype(BF16)
    rim = remote(rim_out, rim_in, r_send, r_recv, d, after)
    rim.start()

    for off in range(1, D):
        send_tile(lax.rem(d + off, D)).wait_send()
    for k in range(D):
        pass_on(k, tiles.at[k]).wait_send()

    @pl.when(d == D - 1)
    def _():
        for q in range(Pn):
            if q % D != D - 1:
                send_stored(q).wait_send()

    for slot in range(slots):
        def drain(slot=slot):
            for off in range(1, D):
                send_ge(slot, lax.rem(d + off, D), slot * D + d).wait_send()
        pl.when(slot * D + d < Pn)(drain)

    rim.wait()
    grad[...] = own[...] + rim_in[...].astype(F32)


def body(probe, positions, object_phase, propagator, stored, measured):
    n = probe.shape[-1]
    sections, rows, columns = object_phase.shape
    assert sections == 1 and rows == n and columns == 2 * n
    Pn = positions.shape[1]
    D = lax.axis_size("depth")
    N = lax.axis_size("lat")
    slots = -(-Pn // D)
    ahead, back = tables(n)
    vmem = pl.BlockSpec(memory_space=pltpu.VMEM)
    smem = pl.BlockSpec(memory_space=pltpu.SMEM)
    dma = pltpu.SemaphoreType.DMA
    leaving, grad = pl.pallas_call(
        functools.partial(kernel, D, N, Pn),
        out_shape=(
            jax.ShapeDtypeStruct((Pn, 2, n, n), BF16),
            jax.ShapeDtypeStruct((2, n, 2 * n), F32),
        ),
        in_specs=[smem] + [vmem] * 7,
        out_specs=(vmem, vmem),
        scratch_shapes=[
            pltpu.VMEM((D, n, 2 * n), BF16),
            pltpu.VMEM((D, n, 2 * n), BF16),
            pltpu.VMEM((2, n, n), F32),
            pltpu.VMEM((Pn, 2 * n, n), BF16),
            pltpu.VMEM((Pn, 2 * n, n), BF16),
            pltpu.VMEM((slots, 2, n, n), BF16),
            pltpu.VMEM((slots, D, 2 * n, n), BF16),
            pltpu.VMEM((Pn, 2 * n, n), BF16),
            pltpu.VMEM((2, n, 2 * n), F32),
            pltpu.VMEM((2, n, 2 * n), F32),
            pltpu.VMEM((2, n, 2 * n), BF16),
            pltpu.VMEM((2, n, 2 * n), BF16),
            dma((D,)), dma((D,)),
            dma((D,)), dma((D,)),
            dma((Pn,)), dma((slots,)),
            dma((slots, D)), dma((Pn,)),
            dma, dma,
        ],
        compiler_params=pltpu.CompilerParams(
            collective_id=0, has_side_effects=True, vmem_limit_bytes=48 << 20),
        cost_estimate=pl.CostEstimate(
            flops=(2 * D * Pn + 4 * D) * 16 * n ** 3, bytes_accessed=32 * n * n * 2 * Pn, transcendentals=0),
    )(positions, ahead, back, probe, object_phase[0], propagator, stored[0], measured)
    return leaving[None], grad[None]


def solution(mesh):
    return jax.shard_map(
        body,
        mesh=mesh,
        in_specs=(
            P(),
            P(None, "lat", None),
            P("depth", "lat", None),
            P(),
            P("depth", "lat", None, None, None),
            P("lat", None, None),
        ),
        out_specs=(P("depth", "lat", None, None, None), P("depth", None, "lat", None)),
        check_vma=False,
    )
```

```python
import functools
import math

import jax
import jax.numpy as jnp
import numpy as np
from jax import lax
from jax.experimental import pallas as pl
from jax.experimental.pallas import tpu as pltpu
from jax.sharding import PartitionSpec as P

MESH = pl.DeviceIdType.MESH
F32 = jnp.float32
BF16 = jnp.bfloat16


def tables(n):
    counter = np.arange(n)
    angles = 2.0 * math.pi / n * (counter[:, None] * counter[None, :] % n)
    re = np.cos(angles) / math.sqrt(n)
    im = -np.sin(angles) / math.sqrt(n)
    ahead = np.block([[re, -im], [im, re]])
    back = np.block([[re, im], [-im, re]])
    return ahead.astype(BF16), back.astype(BF16)


def fit(function, terms):
    top = (math.pi + 1e-3) ** 2
    u = (np.cos(np.pi * (np.arange(400) + 0.5) / 400) + 1) * top / 2
    poly = np.polynomial.Chebyshev.fit(u, function(np.sqrt(u)), terms - 1, domain=[0, top])
    return [float(v) for v in poly.convert(kind=np.polynomial.Polynomial).coef]


SIN = fit(lambda x: np.sin(x) / x, 7)
COS = fit(np.cos, 8)


def horner(coefs, u):
    value = jnp.full_like(u, coefs[-1])
    for coef in coefs[-2::-1]:
        value = value * u + coef
    return value


def cos_sin(x):
    u = x * x
    return horner(COS, u), x * horner(SIN, u)


def rows_to_lanes(x):
    half = x.shape[0] // 2
    return jnp.concatenate([x[:half], x[half:]], axis=1)


def pair(re, im):
    return jnp.concatenate([re.astype(BF16), im.astype(BF16)], axis=0)


def kernel(D, N, Pn, pos, a_hbm, b_hbm, probe_hbm, tile, prop_hbm, stored_hbm, measured_hbm,
           leaving, grad,
           a_ref, b_ref, probe, prop, stored, measured, l_sem, m_sem,
           tiles, nexts, h_ref, waves, rolled, start, st3, ge_out, ge_in, own, nxt, rim_out, rim_in,
           t_send, t_recv, n_send, n_recv, s_send, s_recv, g_send, g_recv, r_send, r_recv):
    n = prop.shape[0]
    slots = st3.shape[0]
    d = lax.axis_index("depth")
    l = lax.axis_index("lat")
    before = lax.rem(l + N - 1, N)
    after = lax.rem(l + 1, N)

    def remote(src, dst, send, recv, depth, lat):
        return pltpu.make_async_remote_copy(
            src_ref=src, dst_ref=dst, send_sem=send, recv_sem=recv,
            device_id=(depth, lat), device_id_type=MESH)

    loads = [
        pltpu.make_async_copy(source, target, l_sem.at[i])
        for i, (source, target) in enumerate((
            (prop_hbm, prop), (probe_hbm, probe), (stored_hbm, stored), (tile, tiles.at[d]),
            (a_hbm, a_ref), (b_hbm, b_ref)))
    ]
    for load in loads:
        load.start()

    def load_measured(slot):
        return pltpu.make_async_copy(
            measured_hbm.at[slot * D + d], measured.at[slot], m_sem.at[slot])

    for slot in range(slots):
        pl.when(slot * D + d < Pn)(lambda slot=slot: load_measured(slot).start())

    barrier = pltpu.get_barrier_semaphore()
    for off in range(1, D):
        pl.semaphore_signal(barrier, inc=1, device_id=(lax.rem(d + off, D), l), device_id_type=MESH)
    for other in (before, after):
        pl.semaphore_signal(barrier, inc=1, device_id=(d, other), device_id_type=MESH)
    pl.semaphore_wait(barrier, D + 1)

    def send_tile(j):
        return remote(tile, tiles.at[d], t_send.at[j], t_recv.at[d], j, l)

    def recv_tile(k):
        return remote(tile, tiles.at[k], t_send.at[k], t_recv.at[k], d, l)

    def pass_on(k, source):
        return remote(source, nexts.at[k], n_send.at[k], n_recv.at[k], d, before)

    def send_stored(q):
        return remote(stored_hbm.at[q], st3.at[q // D], s_send.at[q], s_recv.at[q // D], q % D, l)

    pass_on(d, tile).start()
    for off in range(1, D):
        send_tile(lax.rem(d + off, D)).start()

    @pl.when(d == D - 1)
    def _():
        for q in range(Pn):
            if q % D != D - 1:
                send_stored(q).start()

    loads[0].wait()
    c, s = cos_sin(prop[...])
    h_ref[0] = c
    h_ref[1] = s

    row = lax.broadcasted_iota(jnp.int32, (n, n), 0)
    col = lax.broadcasted_iota(jnp.int32, (n, n), 1)

    def shift(lead, by):
        at = lead + by
        at = jnp.where(at < 0, at + n, at)
        return jnp.where(at >= n, at - n, at)

    def one_hot(where):
        return jnp.where(where, 1.0, 0.0).astype(BF16)

    def move(wave, left, right):
        turned = jnp.dot(wave, right, preferred_element_type=F32).astype(BF16)
        return (jnp.dot(left, turned[:n], preferred_element_type=F32).astype(BF16),
                jnp.dot(left, turned[n:], preferred_element_type=F32).astype(BF16))

    def roll_in(wave, r, c):
        left = one_hot(col == shift(row, -r))
        right = one_hot(row == shift(col, -c))
        return move(wave, left, right)

    def roll_out(wave, r, c):
        left = one_hot(col == shift(row, r))
        right = one_hot(row == shift(col, c))
        return move(wave, left, right)

    loads[1].wait()
    loads[2].wait()

    @pl.loop(0, Pn)
    def _(q):
        re, im = roll_in(probe[...].reshape(2 * n, n), pos[0, q, 0], pos[0, q, 1])
        waves[q, :n] = re
        waves[q, n:] = im
        re, im = roll_in(stored[q].reshape(2 * n, n), pos[1, q, 0], pos[1, q, 1])
        rolled[q, :n] = re
        rolled[q, n:] = im

    for load in loads[3:]:
        load.wait()

    def dft(wave):
        left = jnp.dot(a_ref[...], wave, preferred_element_type=F32).astype(BF16)
        out = jnp.dot(rows_to_lanes(left), b_ref[...], preferred_element_type=F32)
        return out[:, :n], out[:, n:]

    def idft(wave):
        left = jnp.dot(b_ref[...], wave, preferred_element_type=F32).astype(BF16)
        out = jnp.dot(rows_to_lanes(left), a_ref[...], preferred_element_type=F32)
        return out[:, :n], out[:, n:]

    def transmission(k, r, c):
        right = col < c
        here = jnp.where(right, tiles[k, :, n:].astype(F32), tiles[k, :, :n].astype(F32))
        there = jnp.where(right, nexts[k, :, n:].astype(F32), nexts[k, :, :n].astype(F32))
        return cos_sin(jnp.where(row < r, there, here))

    def through(waves_in, ts):
        spectra = [
            dft(pair(re * tr - im * ti, re * ti + im * tr))
            for (re, im), (tr, ti) in zip(waves_in, ts)
        ]
        hr, hi = h_ref[0], h_ref[1]
        return [idft(pair(hr * fr - hi * fi, hr * fi + hi * fr)) for fr, fi in spectra]

    group = 2 if Pn % 2 == 0 else 1

    def forward(k):
        @pl.loop(0, Pn // group)
        def _(i):
            ps = [i * group + j for j in range(group)]
            parts = [waves[p].astype(F32) for p in ps]
            out = through(
                [(part[:n], part[n:]) for part in parts],
                [transmission(k, pos[0, p, 0], pos[0, p, 1]) for p in ps])
            for p, (re, im) in zip(ps, out):
                waves[p] = pair(re, im)

    @pl.loop(0, D + 1)
    def _(k):
        @pl.when((k < D) & (k != d))
        def _():
            recv_tile(k).wait_recv()
            pass_on(k, tiles.at[k]).start()

        @pl.when(k > 0)
        def _():
            pass_on(k - 1, tiles.at[k - 1]).wait_recv()

        @pl.when((k > 0) & (k - 1 < d))
        def _():
            forward(k - 1)

    def send_ge(slot, k, q):
        return remote(ge_out.at[slot, k], ge_in.at[q], g_send.at[slot, k], g_recv.at[q], k, l)

    def backward(slot):
        q = slot * D + d
        r = pos[1, q, 0]
        c = pos[1, q, 1]

        @pl.when(d != D - 1)
        def _():
            remote(stored_hbm.at[q], st3.at[slot], s_send.at[q], s_recv.at[slot], d, l).wait_recv()

        @pl.when(d != D - 1)
        def _():
            re, im = roll_in(st3[slot].reshape(2 * n, n), r, c)
            start[:n] = re
            start[n:] = im

        @pl.when(d == D - 1)
        def _():
            start[...] = rolled[q]

        load_measured(slot).wait()
        wave = start[...].astype(F32)
        xr, xi = through([(wave[:n], wave[n:])], [transmission(D - 1, r, c)])[0]
        fr, fi = dft(pair(xr, xi))
        weight = fr * fr + fi * fi - measured[slot]
        gr, gi = idft(pair(weight * fr, weight * fi))

        def step(i, g):
            k = D - 1 - i
            fr, fi = dft(g)
            hr, hi = h_ref[0], h_ref[1]
            er, ei = idft(pair(hr * fr + hi * fi, hr * fi - hi * fr))
            ge_out[slot, k] = pair(er, ei)

            @pl.when(k == d)
            def _():
                ge_in[q] = pair(er, ei)

            @pl.when(k != d)
            def _():
                send_ge(slot, k, q).start()

            tr, ti = transmission(k, r, c)
            return pair(tr * er + ti * ei, tr * ei - ti * er)

        lax.fori_loop(0, D, step, pair(gr, gi))

    for slot in range(slots):
        if (slot + 1) * D <= Pn:
            backward(slot)
        else:
            pl.when(slot * D + d < Pn)(functools.partial(backward, slot))

    forward(d)

    @pl.loop(0, Pn)
    def _(p):
        re, im = roll_out(waves[p], pos[0, p, 0], pos[0, p, 1])
        leaving[p, 0] = re
        leaving[p, 1] = im

    for q in range(Pn):
        @pl.when(d != q % D)
        def _():
            remote(ge_out.at[0, 0], ge_in.at[q], g_send.at[0, 0], g_recv.at[q], d, l).wait_recv()

        u = rolled[q].astype(F32)
        g = ge_in[q].astype(F32)
        ur, ui, gr, gi = u[:n], u[n:], g[:n], g[n:]
        lower = row < pos[1, q, 0]
        right = col < pos[1, q, 1]
        for part, term in enumerate((ur * gr + ui * gi, ur * gi - ui * gr)):
            here = jnp.where(lower, 0.0, term)
            there = jnp.where(lower, term, 0.0)
            for target, value in ((own, here), (nxt, there)):
                west = jnp.where(right, 0.0, value)
                east = jnp.where(right, value, 0.0)
                if q > 0:
                    west = west + target[part, :, :n]
                    east = east + target[part, :, n:]
                target[part, :, :n] = west
                target[part, :, n:] = east

    rims = []
    for part in range(2):
        for half in range(2):
            at = (part, pl.ds(half * n // 2, n // 2))
            rim_out[at] = nxt[at].astype(BF16)
            i = 2 * part + half
            rims.append((at, remote(
                rim_out.at[at], rim_in.at[at], r_send.at[i], r_recv.at[i], d, after)))
            rims[-1][1].start()

    for off in range(1, D):
        send_tile(lax.rem(d + off, D)).wait_send()
    for k in range(D):
        pass_on(k, tiles.at[k]).wait_send()

    @pl.when(d == D - 1)
    def _():
        for q in range(Pn):
            if q % D != D - 1:
                send_stored(q).wait_send()

    for slot in range(slots):
        def drain(slot=slot):
            for off in range(1, D):
                send_ge(slot, lax.rem(d + off, D), slot * D + d).wait_send()
        pl.when(slot * D + d < Pn)(drain)

    for at, rim in rims:
        rim.wait()
        grad[at] = own[at] + rim_in[at].astype(F32)


def body(probe, positions, object_phase, propagator, stored, measured):
    n = probe.shape[-1]
    sections, rows, columns = object_phase.shape
    assert sections == 1 and rows == n and columns == 2 * n
    Pn = positions.shape[1]
    D = lax.axis_size("depth")
    N = lax.axis_size("lat")
    slots = -(-Pn // D)
    ahead, back = tables(n)
    vmem = pl.BlockSpec(memory_space=pltpu.VMEM)
    hbm = pl.BlockSpec(memory_space=pl.ANY)
    smem = pl.BlockSpec(memory_space=pltpu.SMEM)
    dma = pltpu.SemaphoreType.DMA
    leaving, grad = pl.pallas_call(
        functools.partial(kernel, D, N, Pn),
        out_shape=(
            jax.ShapeDtypeStruct((Pn, 2, n, n), BF16),
            jax.ShapeDtypeStruct((2, n, 2 * n), F32),
        ),
        in_specs=[smem] + [hbm] * 7,
        out_specs=(vmem, vmem),
        scratch_shapes=[
            pltpu.VMEM((2 * n, 2 * n), BF16),
            pltpu.VMEM((2 * n, 2 * n), BF16),
            pltpu.VMEM((2, n, n), BF16),
            pltpu.VMEM((n, n), F32),
            pltpu.VMEM((Pn, 2, n, n), BF16),
            pltpu.VMEM((slots, n, n), F32),
            dma((6,)), dma((slots,)),
            pltpu.VMEM((D, n, 2 * n), BF16),
            pltpu.VMEM((D, n, 2 * n), BF16),
            pltpu.VMEM((2, n, n), F32),
            pltpu.VMEM((Pn, 2 * n, n), BF16),
            pltpu.VMEM((Pn, 2 * n, n), BF16),
            pltpu.VMEM((2 * n, n), BF16),
            pltpu.VMEM((slots, 2, n, n), BF16),
            pltpu.VMEM((slots, D, 2 * n, n), BF16),
            pltpu.VMEM((Pn, 2 * n, n), BF16),
            pltpu.VMEM((2, n, 2 * n), F32),
            pltpu.VMEM((2, n, 2 * n), F32),
            pltpu.VMEM((2, n, 2 * n), BF16),
            pltpu.VMEM((2, n, 2 * n), BF16),
            dma((D,)), dma((D,)),
            dma((D,)), dma((D,)),
            dma((Pn,)), dma((slots,)),
            dma((slots, D)), dma((Pn,)),
            dma((4,)), dma((4,)),
        ],
        compiler_params=pltpu.CompilerParams(
            collective_id=0, has_side_effects=True, vmem_limit_bytes=60 << 20),
        cost_estimate=pl.CostEstimate(
            flops=(2 * D * Pn + 4 * D) * 16 * n ** 3, bytes_accessed=32 * n * n * 2 * Pn, transcendentals=0),
    )(positions, ahead, back, probe, object_phase[0], propagator, stored[0], measured)
    return leaving[None], grad[None]


def solution(mesh):
    return jax.shard_map(
        body,
        mesh=mesh,
        in_specs=(
            P(),
            P(None, "lat", None),
            P("depth", "lat", None),
            P(),
            P("depth", "lat", None, None, None),
            P("lat", None, None),
        ),
        out_specs=(P("depth", "lat", None, None, None), P("depth", None, "lat", None)),
        check_vma=False,
    )
```

```python
import functools
import math

import jax
import jax.numpy as jnp
import numpy as np
from jax import lax
from jax.experimental import pallas as pl
from jax.experimental.pallas import tpu as pltpu
from jax.sharding import PartitionSpec as P

MESH = pl.DeviceIdType.MESH
F32 = jnp.float32
BF16 = jnp.bfloat16


def tables(n):
    counter = np.arange(n)
    angles = 2.0 * math.pi / n * (counter[:, None] * counter[None, :] % n)
    re = np.cos(angles) / math.sqrt(n)
    im = -np.sin(angles) / math.sqrt(n)
    ahead = np.block([[re, -im], [im, re]])
    back = np.block([[re, im], [-im, re]])
    return ahead.astype(BF16), back.astype(BF16)


def fit(function, terms):
    top = (math.pi + 1e-3) ** 2
    u = (np.cos(np.pi * (np.arange(400) + 0.5) / 400) + 1) * top / 2
    poly = np.polynomial.Chebyshev.fit(u, function(np.sqrt(u)), terms - 1, domain=[0, top])
    return [float(v) for v in poly.convert(kind=np.polynomial.Polynomial).coef]


SIN = fit(lambda x: np.sin(x) / x, 7)
COS = fit(np.cos, 8)


def horner(coefs, u):
    value = jnp.full_like(u, coefs[-1])
    for coef in coefs[-2::-1]:
        value = value * u + coef
    return value


def cos_sin(x):
    u = x * x
    return horner(COS, u), x * horner(SIN, u)


def rows_to_lanes(x):
    half = x.shape[0] // 2
    return jnp.concatenate([x[:half], x[half:]], axis=1)


def pair(re, im):
    return jnp.concatenate([re.astype(BF16), im.astype(BF16)], axis=0)


def kernel(D, N, Pn, pos, a_hbm, b_hbm, probe_hbm, tile, prop_hbm, stored_hbm, measured_hbm,
           leaving, grad,
           a_ref, b_ref, probe, prop, stored, measured, l_sem, m_sem,
           tiles, nexts, h_ref, waves, rolled, start, st3, ge_out, ge_in, own, nxt, rim_out, rim_in,
           t_send, t_recv, n_send, n_recv, s_send, s_recv, g_send, g_recv, r_send, r_recv):
    n = prop.shape[0]
    slots = st3.shape[0]
    d = lax.axis_index("depth")
    l = lax.axis_index("lat")
    before = lax.rem(l + N - 1, N)
    after = lax.rem(l + 1, N)

    def remote(src, dst, send, recv, depth, lat):
        return pltpu.make_async_remote_copy(
            src_ref=src, dst_ref=dst, send_sem=send, recv_sem=recv,
            device_id=(depth, lat), device_id_type=MESH)

    loads = [
        pltpu.make_async_copy(source, target, l_sem.at[i])
        for i, (source, target) in enumerate((
            (prop_hbm, prop), (probe_hbm, probe), (stored_hbm, stored), (tile, tiles.at[d]),
            (a_hbm, a_ref), (b_hbm, b_ref)))
    ]
    for load in loads:
        load.start()

    def load_measured(slot):
        return pltpu.make_async_copy(
            measured_hbm.at[slot * D + d], measured.at[slot], m_sem.at[slot])

    for slot in range(slots):
        pl.when(slot * D + d < Pn)(lambda slot=slot: load_measured(slot).start())

    barrier = pltpu.get_barrier_semaphore()
    for off in range(1, D):
        pl.semaphore_signal(barrier, inc=1, device_id=(lax.rem(d + off, D), l), device_id_type=MESH)
    for other in (before, after):
        pl.semaphore_signal(barrier, inc=1, device_id=(d, other), device_id_type=MESH)
    pl.semaphore_wait(barrier, D + 1)

    half = n // 2
    spans = [pl.ds(h * half, half) for h in range(2)]

    def send_tile(j, h):
        return remote(tile.at[spans[h]], tiles.at[d, spans[h]],
                      t_send.at[j, h], t_recv.at[d, h], j, l)

    def recv_tile(k, h):
        return remote(tile.at[spans[h]], tiles.at[k, spans[h]],
                      t_send.at[k, h], t_recv.at[k, h], d, l)

    def pass_on(k, h, source=None):
        source = tiles.at[k, spans[h]] if source is None else source.at[spans[h]]
        return remote(source, nexts.at[k, spans[h]], n_send.at[k, h], n_recv.at[k, h], d, before)

    def send_stored(q):
        return remote(stored_hbm.at[q], st3.at[q // D], s_send.at[q], s_recv.at[q // D], q % D, l)

    for h in range(2):
        pass_on(d, h, tile).start()
        for off in range(1, D):
            send_tile(lax.rem(d + off, D), h).start()

    @pl.when(d == D - 1)
    def _():
        for q in range(Pn):
            if q % D != D - 1:
                send_stored(q).start()

    loads[0].wait()
    c, s = cos_sin(prop[...])
    h_ref[0] = c
    h_ref[1] = s

    row = lax.broadcasted_iota(jnp.int32, (n, n), 0)
    col = lax.broadcasted_iota(jnp.int32, (n, n), 1)

    def shift(lead, by):
        at = lead + by
        at = jnp.where(at < 0, at + n, at)
        return jnp.where(at >= n, at - n, at)

    def one_hot(where):
        return jnp.where(where, 1.0, 0.0).astype(BF16)

    def move(wave, left, right):
        turned = jnp.dot(wave, right, preferred_element_type=F32).astype(BF16)
        return (jnp.dot(left, turned[:n], preferred_element_type=F32).astype(BF16),
                jnp.dot(left, turned[n:], preferred_element_type=F32).astype(BF16))

    def roll_in(wave, r, c):
        left = one_hot(col == shift(row, -r))
        right = one_hot(row == shift(col, -c))
        return move(wave, left, right)

    def roll_out(wave, r, c):
        left = one_hot(col == shift(row, r))
        right = one_hot(row == shift(col, c))
        return move(wave, left, right)

    loads[1].wait()
    loads[2].wait()

    @pl.loop(0, Pn)
    def _(q):
        re, im = roll_in(probe[...].reshape(2 * n, n), pos[0, q, 0], pos[0, q, 1])
        waves[q, :n] = re
        waves[q, n:] = im
        re, im = roll_in(stored[q].reshape(2 * n, n), pos[1, q, 0], pos[1, q, 1])
        rolled[q, :n] = re
        rolled[q, n:] = im

    for load in loads[3:]:
        load.wait()

    def dft(wave):
        left = jnp.dot(a_ref[...], wave, preferred_element_type=F32).astype(BF16)
        out = jnp.dot(rows_to_lanes(left), b_ref[...], preferred_element_type=F32)
        return out[:, :n], out[:, n:]

    def idft(wave):
        left = jnp.dot(b_ref[...], wave, preferred_element_type=F32).astype(BF16)
        out = jnp.dot(rows_to_lanes(left), a_ref[...], preferred_element_type=F32)
        return out[:, :n], out[:, n:]

    def transmission(k, r, c):
        right = col < c
        here = jnp.where(right, tiles[k, :, n:].astype(F32), tiles[k, :, :n].astype(F32))
        there = jnp.where(right, nexts[k, :, n:].astype(F32), nexts[k, :, :n].astype(F32))
        return cos_sin(jnp.where(row < r, there, here))

    def through(waves_in, ts):
        spectra = [
            dft(pair(re * tr - im * ti, re * ti + im * tr))
            for (re, im), (tr, ti) in zip(waves_in, ts)
        ]
        hr, hi = h_ref[0], h_ref[1]
        return [idft(pair(hr * fr - hi * fi, hr * fi + hi * fr)) for fr, fi in spectra]

    group = 2 if Pn % 2 == 0 else 1

    def forward(k):
        @pl.loop(0, Pn // group)
        def _(i):
            ps = [i * group + j for j in range(group)]
            parts = [waves[p].astype(F32) for p in ps]
            out = through(
                [(part[:n], part[n:]) for part in parts],
                [transmission(k, pos[0, p, 0], pos[0, p, 1]) for p in ps])
            for p, (re, im) in zip(ps, out):
                waves[p] = pair(re, im)

    @pl.loop(0, D)
    def _(k):
        @pl.when(k != d)
        def _():
            recv_tile(k, 0).wait_recv()
            pass_on(k, 0).start()

    @pl.loop(0, D + 1)
    def _(k):
        @pl.when((k < D) & (k != d))
        def _():
            recv_tile(k, 1).wait_recv()
            pass_on(k, 1).start()

        @pl.when(k > 0)
        def _():
            for h in range(2):
                pass_on(k - 1, h).wait_recv()

        @pl.when((k > 0) & (k - 1 < d))
        def _():
            forward(k - 1)

    def send_ge(slot, k, q, h):
        return remote(ge_out.at[slot, k, h], ge_in.at[q, h],
                      g_send.at[slot, k, h], g_recv.at[q, h], k, l)

    def backward(slot):
        q = slot * D + d
        r = pos[1, q, 0]
        c = pos[1, q, 1]

        @pl.when(d != D - 1)
        def _():
            remote(stored_hbm.at[q], st3.at[slot], s_send.at[q], s_recv.at[slot], d, l).wait_recv()

        @pl.when(d != D - 1)
        def _():
            re, im = roll_in(st3[slot].reshape(2 * n, n), r, c)
            start[:n] = re
            start[n:] = im

        @pl.when(d == D - 1)
        def _():
            start[...] = rolled[q]

        load_measured(slot).wait()
        wave = start[...].astype(F32)
        xr, xi = through([(wave[:n], wave[n:])], [transmission(D - 1, r, c)])[0]
        fr, fi = dft(pair(xr, xi))
        weight = fr * fr + fi * fi - measured[slot]
        gr, gi = idft(pair(weight * fr, weight * fi))

        def step(i, g):
            k = D - 1 - i
            fr, fi = dft(g)
            hr, hi = h_ref[0], h_ref[1]
            er, ei = idft(pair(hr * fr + hi * fi, hr * fi - hi * fr))
            pieces = [(h, part, value[h * half:(h + 1) * half].astype(BF16))
                      for h in range(2) for part, value in enumerate((er, ei))]

            @pl.when(k == d)
            def _():
                for h, part, value in pieces:
                    ge_in[q, h, part] = value

            @pl.when(k != d)
            def _():
                for h, part, value in pieces:
                    ge_out[slot, k, h, part] = value
                send_ge(slot, k, q, 0).start()

            tr, ti = transmission(k, r, c)
            return pair(tr * er + ti * ei, tr * ei - ti * er)

        lax.fori_loop(0, D, step, pair(gr, gi))

        for k in reversed(range(D)):
            pl.when(k != d)(lambda k=k: send_ge(slot, k, q, 1).start())

    for slot in range(slots):
        if (slot + 1) * D <= Pn:
            backward(slot)
        else:
            pl.when(slot * D + d < Pn)(functools.partial(backward, slot))

    forward(d)

    @pl.loop(0, Pn)
    def _(p):
        re, im = roll_out(waves[p], pos[0, p, 0], pos[0, p, 1])
        leaving[p, 0] = re
        leaving[p, 1] = im

    rims = []
    for h in range(2):
        at, lines = spans[h], slice(h * half, (h + 1) * half)
        for q in range(Pn):
            @pl.when(d != q % D)
            def _():
                remote(ge_out.at[0, 0, h], ge_in.at[q, h],
                       g_send.at[0, 0, h], g_recv.at[q, h], d, l).wait_recv()

            ur = rolled[q, lines].astype(F32)
            ui = rolled[q, n + h * half:n + (h + 1) * half].astype(F32)
            gr, gi = ge_in[q, h, 0].astype(F32), ge_in[q, h, 1].astype(F32)
            lower = row[lines] < pos[1, q, 0]
            right = col[lines] < pos[1, q, 1]
            for part, term in enumerate((ur * gr + ui * gi, ur * gi - ui * gr)):
                here = jnp.where(lower, 0.0, term)
                there = jnp.where(lower, term, 0.0)
                for target, value in ((own, here), (nxt, there)):
                    west = jnp.where(right, 0.0, value)
                    east = jnp.where(right, value, 0.0)
                    if q > 0:
                        west = west + target[part, lines, :n]
                        east = east + target[part, lines, n:]
                    target[part, lines, :n] = west
                    target[part, lines, n:] = east

        for part in range(2):
            rim_out[part, lines] = nxt[part, lines].astype(BF16)
            rims.append(((part, lines), remote(
                rim_out.at[part, at], rim_in.at[part, at],
                r_send.at[part, h], r_recv.at[part, h], d, after)))
            rims[-1][1].start()

    for off in range(1, D):
        for h in range(2):
            send_tile(lax.rem(d + off, D), h).wait_send()
    for k in range(D):
        for h in range(2):
            pass_on(k, h).wait_send()

    @pl.when(d == D - 1)
    def _():
        for q in range(Pn):
            if q % D != D - 1:
                send_stored(q).wait_send()

    for slot in range(slots):
        def drain(slot=slot):
            for off in range(1, D):
                for h in range(2):
                    send_ge(slot, lax.rem(d + off, D), slot * D + d, h).wait_send()
        pl.when(slot * D + d < Pn)(drain)

    for at, rim in rims:
        rim.wait()
        grad[at] = own[at] + rim_in[at].astype(F32)


def body(probe, positions, object_phase, propagator, stored, measured):
    n = probe.shape[-1]
    sections, rows, columns = object_phase.shape
    assert sections == 1 and rows == n and columns == 2 * n
    Pn = positions.shape[1]
    D = lax.axis_size("depth")
    N = lax.axis_size("lat")
    slots = -(-Pn // D)
    ahead, back = tables(n)
    vmem = pl.BlockSpec(memory_space=pltpu.VMEM)
    hbm = pl.BlockSpec(memory_space=pl.ANY)
    smem = pl.BlockSpec(memory_space=pltpu.SMEM)
    dma = pltpu.SemaphoreType.DMA
    leaving, grad = pl.pallas_call(
        functools.partial(kernel, D, N, Pn),
        out_shape=(
            jax.ShapeDtypeStruct((Pn, 2, n, n), BF16),
            jax.ShapeDtypeStruct((2, n, 2 * n), F32),
        ),
        in_specs=[smem] + [hbm] * 7,
        out_specs=(vmem, vmem),
        scratch_shapes=[
            pltpu.VMEM((2 * n, 2 * n), BF16),
            pltpu.VMEM((2 * n, 2 * n), BF16),
            pltpu.VMEM((2, n, n), BF16),
            pltpu.VMEM((n, n), F32),
            pltpu.VMEM((Pn, 2, n, n), BF16),
            pltpu.VMEM((slots, n, n), F32),
            dma((6,)), dma((slots,)),
            pltpu.VMEM((D, n, 2 * n), BF16),
            pltpu.VMEM((D, n, 2 * n), BF16),
            pltpu.VMEM((2, n, n), F32),
            pltpu.VMEM((Pn, 2 * n, n), BF16),
            pltpu.VMEM((Pn, 2 * n, n), BF16),
            pltpu.VMEM((2 * n, n), BF16),
            pltpu.VMEM((slots, 2, n, n), BF16),
            pltpu.VMEM((slots, D, 2, 2, n // 2, n), BF16),
            pltpu.VMEM((Pn, 2, 2, n // 2, n), BF16),
            pltpu.VMEM((2, n, 2 * n), F32),
            pltpu.VMEM((2, n, 2 * n), F32),
            pltpu.VMEM((2, n, 2 * n), BF16),
            pltpu.VMEM((2, n, 2 * n), BF16),
            dma((D, 2)), dma((D, 2)),
            dma((D, 2)), dma((D, 2)),
            dma((Pn,)), dma((slots,)),
            dma((slots, D, 2)), dma((Pn, 2)),
            dma((2, 2)), dma((2, 2)),
        ],
        compiler_params=pltpu.CompilerParams(
            collective_id=0, has_side_effects=True, vmem_limit_bytes=60 << 20),
        cost_estimate=pl.CostEstimate(
            flops=(2 * D * Pn + 4 * D) * 16 * n ** 3, bytes_accessed=32 * n * n * 2 * Pn, transcendentals=0),
    )(positions, ahead, back, probe, object_phase[0], propagator, stored[0], measured)
    return leaving[None], grad[None]


def solution(mesh):
    return jax.shard_map(
        body,
        mesh=mesh,
        in_specs=(
            P(),
            P(None, "lat", None),
            P("depth", "lat", None),
            P(),
            P("depth", "lat", None, None, None),
            P("lat", None, None),
        ),
        out_specs=(P("depth", "lat", None, None, None), P("depth", None, "lat", None)),
        check_vma=False,
    )
```
